32 devices in a mesh: tm: 8 (over z, x), inner: 4 (over y, core).
Axes of the slice: x: 2, y: 2, z: 4, core: 2. Of those that a mesh axis runs over, the one named last changes fastest.
Arguments:
- start_panels: float32 [8, 192, 2048], P('tm', None, 'inner'), may hold values from -6 to 6
- kinetic: float32 [2048, 2048], P('inner')
- fields: int32 [8, 2048], P('tm'), may hold values from -1 to 1, as said below
Outputs:
- orbitals: float32 [8, 4, 192, 2048], P('tm', None, None, 'inner')
- log_scales: float32 [8, 4, 192], P('tm')
The draws below stay inside these ranges and needn't reach their ends.
Inputs may be any that keep to these rules, and one draw needn't show every extreme that they name: `fields`: each entry is -1 or +1.
All inputs are finite; a program needn't handle non-finite values.
Results may differ from the reference program's by a relative error of at most 0.0003.
Values sent between devices are 32-bit elements; how exact they have to be, the bound alone decides.
A program may use at most 128 MiB of HBM per device.

```python
import math
import jax
import jax.numpy as jnp
from jax import lax

N = 2048
R = 192
L_DEV = 1
SLICES = 8
HOPS = 4
N_TM = 8


def draw_kinetic(key, part):
    noise = jnp.clip(jax.random.normal(key, (N, N), jnp.float32), -4.0, 4.0)
    return jnp.eye(N, dtype=jnp.float32) + 0.2 / math.sqrt(N) * noise


def draw_fields(key, part):
    return 2 * jax.random.randint(key, (SLICES, N), 0, 2, dtype=jnp.int32) - 1


def levels(stream_key, extent, cuts, smallest, high):
    gain, own = 1.0, jax.random.fold_in(stream_key, 6)
    for dim, parts in cuts:
        draws = jnp.exp(jax.random.uniform(jax.random.fold_in(own, dim), (parts,), jnp.float32, smallest / len(cuts), high / len(cuts)))
        gain = gain * jnp.repeat(draws, extent[dim] // parts).reshape([-1 if axis == dim else 1 for axis in range(len(extent))])
    return gain


def centred(own_key, dims, spread, bound, shards=(), kind=jnp.bfloat16):
    result = spread * jax.random.normal(own_key, dims, jnp.float32)
    if shards:
        result = result * levels(own_key, dims, shards, -0.22, 0.18)
    return jnp.clip(result, -bound, bound).astype(kind)


def setup_inputs(seed: int = 0) -> dict:
    keys = jax.random.split(jax.random.key(seed), 4)
    return {
        "start_panels": centred(keys[0], (N_TM, R, N), 1.0, 6.0, ((0, 8), (2, 4)), jnp.float32),
        "kinetic": draw_kinetic(jax.random.fold_in(keys[3], 71), 0),
        "fields": draw_fields(jax.random.fold_in(keys[3], 71), 0),
    }


coupling = 0.17725

def reference(start_panels, kinetic, fields):
    highest = lax.Precision.HIGHEST
    scales = jnp.exp(coupling * fields.astype(jnp.float32)).reshape(N_TM, L_DEV, N)
    state = start_panels
    orbit_list = []
    log_list = []
    for hop in range(HOPS):
        for layer in range(L_DEV):
            state = jnp.einsum('gcj,ij->gci', state, kinetic, precision=highest) * scales[:, layer][:, None, :]
        gram_matrix = jnp.einsum('gcj,gdj->gcd', state, state, precision=highest)
        lower = jnp.linalg.cholesky(gram_matrix)
        orthonormal = lax.linalg.triangular_solve(lower, state, left_side=True, lower=True)
        orbit_list.append(math.sqrt(N) * orthonormal)
        log_list.append(jnp.log(jnp.diagonal(lower, axis1=1, axis2=2)))
        state = jnp.roll(orthonormal, 1, axis=0)
    return (jnp.stack(orbit_list, axis=1), jnp.stack(log_list, axis=1))
```

```python
import functools
import math

import jax
import jax.numpy as jnp
from jax import lax
from jax.experimental import pallas as pl
from jax.experimental.pallas import tpu as pltpu
from jax.sharding import PartitionSpec as P

coupling = 0.17725
LANES = 128
B = 8


def from_behind(block, axis, distance):
    n = lax.axis_size(axis)
    distance %= n
    if distance == 0:
        return block
    return lax.ppermute(block, axis, [((i - distance) % n, i) for i in range(n)])


def contract(left, right, dims, precision):
    return lax.dot_general(
        left,
        right,
        (dims, ((), ())),
        precision=precision,
        preferred_element_type=jnp.float32,
    )


HIGHEST = lax.Precision.HIGHEST


def factor_into(work, columns):
    r, width = work.shape
    tiles = width // LANES
    lane = lax.broadcasted_iota(jnp.int32, (1, LANES), 1)
    lane_all = lax.broadcasted_iota(jnp.int32, (1, width), 1)
    diagonal = [jnp.ones((1, LANES), jnp.float32) for _ in range(tiles)]
    for p in range(0, r, B):
        home, off = p // LANES, p % LANES
        block = work[p : p + B, home * LANES : (home + 1) * LANES]
        for j in range(B):
            columns[j * B : (j + 1) * B, :] = jnp.broadcast_to(
                block[:, off + j : off + j + 1], (B, LANES)
            )
        d = [[columns[j * B + i : j * B + i + 1, :] for j in range(i + 1)] for i in range(B)]
        rows = []
        for t in range(B):
            parts = [work[p + t : p + t + 1, q * LANES : (q + 1) * LANES] for q in range(tiles)]
            unit = (lane == off + t).astype(jnp.float32)
            parts[home] = jnp.where((lane >= off) & (lane < off + B), unit, parts[home])
            rows.append(parts)
        for t in range(B):
            inverse = lax.rsqrt(d[t][t])
            diagonal[home] = jnp.where(lane == off + t, inverse, diagonal[home])
            below = [d[s][t] * inverse for s in range(t + 1, B)]
            for s in range(t + 1, B):
                for u in range(t + 1, s + 1):
                    d[s][u] = d[s][u] - below[s - t - 1] * below[u - t - 1]
            rows[t] = [part * inverse for part in rows[t]]
            for s in range(t + 1, B):
                rows[s] = [a - below[s - t - 1] * b for a, b in zip(rows[s], rows[t])]
        for t in range(B):
            for q in range(tiles):
                work[p + t : p + t + 1, q * LANES : (q + 1) * LANES] = rows[t][q]
        if p + B < r:
            pivot = work[p : p + B, :]
            turned = pivot.T[p + B : r, :]
            change = contract(turned, pivot, ((1,), (0,)), HIGHEST)
            rest = work[p + B : r, :]
            rest = jnp.where((lane_all >= p) & (lane_all < p + B), 0.0, rest)
            work[p + B : r, :] = rest - change
    return jnp.concatenate(diagonal, axis=1)


def factor_kernel(gram, inverse, logs, work, columns):
    r = gram.shape[0]
    work[...] = jnp.zeros_like(work)
    work[:, :r] = gram[...]
    diagonal = factor_into(work, columns)
    logs[...] = -jnp.log(diagonal[:, :r])
    below = lax.broadcasted_iota(jnp.int32, (r, r), 0) >= lax.broadcasted_iota(
        jnp.int32, (r, r), 1
    )
    inverse[...] = jnp.where(below, work[:, :r], 0.0)


def factor(gram):
    r = gram.shape[0]
    width = -(-r // LANES) * LANES
    return pl.pallas_call(
        factor_kernel,
        out_shape=(
            jax.ShapeDtypeStruct((r, r), jnp.float32),
            jax.ShapeDtypeStruct((1, r), jnp.float32),
        ),
        in_specs=[pl.BlockSpec(memory_space=pltpu.VMEM)],
        out_specs=(pl.BlockSpec(memory_space=pltpu.VMEM),) * 2,
        scratch_shapes=[
            pltpu.VMEM((r, width), jnp.float32),
            pltpu.VMEM((B * B, LANES), jnp.float32),
        ],
        compiler_params=pltpu.CompilerParams(vmem_limit_bytes=16 * 2**20),
        cost_estimate=pl.CostEstimate(
            flops=10**10, bytes_accessed=3 * 4 * r * r, transcendentals=2 * r
        ),
        name="factor",
    )(gram)


def on_device(start_panels, kinetic, fields):
    rows, sites = kinetic.shape
    r = start_panels.shape[1]
    rank = lax.axis_index("inner")
    hops = lax.axis_size("tm") // 2
    first = rank * rows
    own_fields = lax.dynamic_slice_in_dim(fields, first, rows, 1)

    def mapped(panel, hop):
        scale = jnp.exp(coupling * from_behind(own_fields, "tm", -hop).astype(jnp.float32))
        return contract(panel, kinetic, ((1,), (1,)), lax.Precision.HIGH) * scale

    def gathered(block):
        return lax.all_gather(block, "inner", axis=1, tiled=True)

    def own(panel):
        return lax.dynamic_slice_in_dim(panel, first, rows, 1)

    gain = math.sqrt(sites)
    orbit_list, log_list = [], []
    panel = gathered(mapped(gathered(start_panels[0]), 0))
    for hop in range(hops):
        gram = contract(panel, panel, ((1,), (1,)), HIGHEST)
        if hop + 1 < hops:
            ahead = gathered(mapped(panel, hop + 1))
            inverse, logs = factor(gram)
            out = contract(gain * inverse, own(panel), ((1,), (0,)), HIGHEST)
            orbit_list.append(from_behind(out, "tm", hop))
            log_list.append(from_behind(logs, "tm", hop))
            panel = contract(inverse, ahead, ((1,), (0,)), HIGHEST)
        else:
            moved = from_behind(own(panel), "tm", hop)
            inverse, logs = factor(from_behind(gram, "tm", hop))
            orbit_list.append(contract(gain * inverse, moved, ((1,), (0,)), HIGHEST))
            log_list.append(logs)
    return (
        jnp.stack(orbit_list, 0)[None],
        jnp.concatenate(log_list, 0)[None],
    )


def solution(mesh):
    placed = (P("tm", None, "inner"), P("inner", None), P("tm", None))
    return jax.shard_map(
        on_device,
        mesh=mesh,
        in_specs=placed,
        out_specs=(P("tm", None, None, "inner"), P("tm", None, None)),
        check_vma=False,
    )
```

```python
import functools
import math

import jax
import jax.numpy as jnp
from jax import lax
from jax.experimental import pallas as pl
from jax.experimental.pallas import tpu as pltpu
from jax.sharding import PartitionSpec as P

coupling = 0.17725
LANES = 128
B = 8


def contract(left, right, dims, precision):
    return lax.dot_general(
        left,
        right,
        (dims, ((), ())),
        precision=precision,
        preferred_element_type=jnp.float32,
    )


HIGHEST = lax.Precision.HIGHEST


def factor_into(work, columns, midway=None):
    r, width = work.shape
    tiles = width // LANES
    lane = lax.broadcasted_iota(jnp.int32, (1, LANES), 1)
    lane_all = lax.broadcasted_iota(jnp.int32, (1, width), 1)
    diagonal = [jnp.ones((1, LANES), jnp.float32) for _ in range(tiles)]
    for p in range(0, r, B):
        if midway is not None and p == (r * 3 // 4) // B * B:
            midway()
        home, off = p // LANES, p % LANES
        block = work[p : p + B, home * LANES : (home + 1) * LANES]
        for j in range(B):
            columns[j * B : (j + 1) * B, :] = jnp.broadcast_to(
                block[:, off + j : off + j + 1], (B, LANES)
            )
        d = [[columns[j * B + i : j * B + i + 1, :] for j in range(i + 1)] for i in range(B)]
        rows = []
        for t in range(B):
            parts = [work[p + t : p + t + 1, q * LANES : (q + 1) * LANES] for q in range(tiles)]
            unit = (lane == off + t).astype(jnp.float32)
            parts[home] = jnp.where((lane >= off) & (lane < off + B), unit, parts[home])
            rows.append(parts)
        for t in range(B):
            inverse = lax.rsqrt(d[t][t])
            diagonal[home] = jnp.where(lane == off + t, inverse, diagonal[home])
            below = [d[s][t] * inverse for s in range(t + 1, B)]
            for s in range(t + 1, B):
                for u in range(t + 1, s + 1):
                    d[s][u] = d[s][u] - below[s - t - 1] * below[u - t - 1]
            rows[t] = [part * inverse for part in rows[t]]
            for s in range(t + 1, B):
                rows[s] = [a - below[s - t - 1] * b for a, b in zip(rows[s], rows[t])]
        for t in range(B):
            for q in range(tiles):
                work[p + t : p + t + 1, q * LANES : (q + 1) * LANES] = rows[t][q]
        if p + B < r:
            pivot = work[p : p + B, :]
            turned = pivot.T[p + B : r, :]
            change = contract(turned, pivot, ((1,), (0,)), HIGHEST)
            rest = work[p + B : r, :]
            rest = jnp.where((lane_all >= p) & (lane_all < p + B), 0.0, rest)
            work[p + B : r, :] = rest - change
    return jnp.concatenate(diagonal, axis=1)


HIGH = lax.Precision.HIGH
MESH = pl.DeviceIdType.MESH


def split(value):
    high = value.astype(jnp.bfloat16)
    return high, (value - high.astype(jnp.float32)).astype(jnp.bfloat16)


def chain_kernel(
    n_tm,
    n_inner,
    hops,
    start,
    kinetic,
    fields,
    orbits,
    logs,
    full,
    panel,
    kin,
    kin_high,
    kin_low,
    scales,
    stage,
    log_stage,
    log_in,
    gram_out,
    gram_in,
    moved,
    inverse,
    work,
    columns,
    ag_send,
    ag_recv,
    far_send,
    far_recv,
    local,
):
    r, rows = start.shape
    sites = n_inner * rows
    chips = n_inner // 2
    gain = math.sqrt(sites)
    last = hops - 1
    tm = lax.axis_index("tm")
    me = lax.axis_index("inner")
    chip, core = me // 2, me % 2
    sibling = chip * 2 + (1 - core)
    across = [((chip + d) % chips) * 2 + core for d in range(1, chips)]
    origin = [((chip + chips - d) % chips) * 2 + core for d in range(1, chips)]

    def ahead(distance):
        return lax.rem(tm + distance + n_tm, n_tm)

    offsets = sorted({d % n_tm for k in range(1, hops) for d in (k, -k)})
    barrier = pltpu.get_barrier_semaphore()
    for peer in [sibling] + across:
        pl.semaphore_signal(barrier, inc=1, device_id={"inner": peer}, device_id_type=MESH)
    for d in offsets:
        pl.semaphore_signal(barrier, inc=1, device_id={"tm": ahead(d)}, device_id_type=MESH)
    load_kin = pltpu.make_async_copy(kinetic, kin, local.at[0])
    load_kin.start()
    load_start = pltpu.make_async_copy(start, full.at[0, me], local.at[1])
    load_start.start()
    own_fields = fields[:, pl.ds(pl.multiple_of(me * rows, rows), rows)]
    scales[0] = jnp.broadcast_to(jnp.exp(coupling * own_fields.astype(jnp.float32)), (8, rows))
    load_start.wait()
    pl.semaphore_wait(barrier, chips + len(offsets))

    def send(source, target, sems, device):
        return pltpu.make_async_remote_copy(
            src_ref=source,
            dst_ref=target,
            send_sem=sems[0],
            recv_sem=sems[1],
            device_id=device,
            device_id_type=MESH,
        )

    def gather(g):
        def sems(i):
            return ag_send.at[g, i], ag_recv.at[g, i]

        def block(slot, i, device):
            return send(full.at[g, slot], full.at[g, slot], sems(i), {"inner": device})

        crossing = [block(me, d, across[d - 1]) for d in range(1, chips)]
        beside = block(me, 0, sibling)
        passed = [block(origin[d - 1], chips - 1 + d, sibling) for d in range(1, chips)]
        for copy in crossing:
            copy.start()
        beside.start()

        def forward():
            for copy, onward in zip(crossing, passed):
                copy.wait_recv()
                onward.start()

        def finish():
            beside.wait()
            for copy in crossing:
                copy.wait_send()
            for copy in passed:
                copy.wait()

        return forward, finish

    def far(kind, k):
        return far_send.at[kind, k], far_recv.at[kind, k]

    def mapped(blocks, hop):
        total = jnp.zeros((r, rows), jnp.float32)
        for j in range(n_inner):
            high, low = split(blocks[j])
            dims = ((1,), (0,))
            total += contract(high, kin_high[j], dims, None)
            total += contract(high, kin_low[j], dims, None)
            total += contract(low, kin_high[j], dims, None)
        return total * scales[hop][0:1, :]

    def gram_of(blocks):
        total = jnp.zeros((r, r), jnp.float32)
        for j in range(n_inner):
            block = blocks[j]
            total += contract(block, block, ((1,), (1,)), HIGHEST)
        return total

    below = lax.broadcasted_iota(jnp.int32, (r, r), 0) >= lax.broadcasted_iota(
        jnp.int32, (r, r), 1
    )

    def factor(midway=None):
        diagonal = factor_into(work, columns, midway)
        inverse[...] = jnp.where(below, work[:, :r], 0.0)
        return -jnp.log(diagonal)

    pending = []
    forward, finish = gather(0)
    for k in range(1, hops):
        copy = send(scales.at[0], scales.at[k], far(0, k), {"tm": ahead(-k)})
        copy.start()
        pending.append(copy)
    load_kin.wait()
    for j in range(n_inner):
        turned = kin[:, j * rows : (j + 1) * rows].T
        kin_high[j], kin_low[j] = split(turned)
    forward()
    finish()
    full[1, me] = mapped(full.at[0], 0)
    forward, finish = gather(1)
    for copy in pending:
        copy.wait()
    pending = []
    forward()
    finish()

    blocks = full.at[1]
    work[...] = jnp.zeros_like(work)
    for hop in range(hops):
        if hop < last:
            full[hop + 2, me] = mapped(blocks, hop + 1)
            forward, finish = gather(hop + 2)
            work[:, :r] = gram_of(blocks)
            log_stage[hop] = jnp.broadcast_to(factor(forward), log_stage.shape[1:])
            stage[hop] = contract(gain * inverse[...], blocks[me], ((1,), (0,)), HIGH)
            if hop == 0:
                copy = pltpu.make_async_copy(stage.at[0], orbits.at[0], local.at[2])
                copy.start()
                pending.append(copy)
            else:
                there = {"tm": ahead(hop)}
                copy = send(stage.at[hop], orbits.at[hop], far(1, hop), there)
                copy.start()
                pending.append(copy)
                copy = send(log_stage.at[hop], log_in.at[hop], far(2, hop), there)
                copy.start()
                pending.append(copy)
            finish()
            for j in range(n_inner):
                panel[j] = contract(inverse[...], full[hop + 2, j], ((1,), (0,)), HIGH)
            blocks = panel
        else:
            there = {"tm": ahead(last)}
            half = r // 2
            part = pl.ds(pl.multiple_of(core * half, 8), half)
            gram_out[:, :r] = gram_of(blocks)
            gram_out[:, r:] = jnp.zeros((r, gram_out.shape[1] - r), jnp.float32)
            shift = send(gram_out.at[part], gram_in.at[part], far(3, 0), there)
            shift.start()
            carry = send(panel.at[me], moved, far(3, 1), there)
            carry.start()
            shift.wait_recv()
            swap = send(gram_in.at[part], gram_in.at[part], far(3, 2), {"inner": sibling})
            swap.start()
            swap.wait()
            work[...] = gram_in[...]
            log_stage[hop] = jnp.broadcast_to(factor(), log_stage.shape[1:])
            shift.wait_send()
            carry.wait()
            stage[hop] = contract(gain * inverse[...], moved[...], ((1,), (0,)), HIGH)
            copy = pltpu.make_async_copy(stage.at[hop], orbits.at[hop], local.at[3])
            copy.start()
            pending.append(copy)
    for copy in pending:
        copy.wait()
    for hop in range(hops):
        held = log_stage if hop in (0, last) else log_in
        logs[hop : hop + 1, :] = held[hop][0:1, :r]


def on_device(start_panels, kinetic, fields):
    rows, sites = kinetic.shape
    r = start_panels.shape[1]
    n_tm, n_inner = lax.axis_size("tm"), lax.axis_size("inner")
    hops = n_tm // 2
    width = -(-r // LANES) * LANES
    f32, bf16 = jnp.float32, jnp.bfloat16
    vmem, anywhere = pl.BlockSpec(memory_space=pltpu.VMEM), pl.BlockSpec(memory_space=pl.ANY)
    orbits, logs = pl.pallas_call(
        functools.partial(chain_kernel, n_tm, n_inner, hops),
        out_shape=(
            jax.ShapeDtypeStruct((hops, r, rows), f32),
            jax.ShapeDtypeStruct((hops, r), f32),
        ),
        in_specs=[anywhere, anywhere, vmem],
        out_specs=(anywhere, vmem),
        scratch_shapes=[
            pltpu.VMEM((hops + 1, n_inner, r, rows), f32),
            pltpu.VMEM((n_inner, r, rows), f32),
            pltpu.VMEM((rows, sites), f32),
            pltpu.VMEM((n_inner, rows, rows), bf16),
            pltpu.VMEM((n_inner, rows, rows), bf16),
            pltpu.VMEM((hops, 8, rows), f32),
            pltpu.VMEM((hops, r, rows), f32),
            pltpu.VMEM((hops, 8, width), f32),
            pltpu.VMEM((hops, 8, width), f32),
            pltpu.VMEM((r, width), f32),
            pltpu.VMEM((r, width), f32),
            pltpu.VMEM((r, rows), f32),
            pltpu.VMEM((r, r), f32),
            pltpu.VMEM((r, width), f32),
            pltpu.VMEM((B * B, LANES), f32),
            pltpu.SemaphoreType.DMA((hops + 1, n_inner)),
            pltpu.SemaphoreType.DMA((hops + 1, n_inner)),
            pltpu.SemaphoreType.DMA((4, max(hops, 3))),
            pltpu.SemaphoreType.DMA((4, max(hops, 3))),
            pltpu.SemaphoreType.DMA((4,)),
        ],
        compiler_params=pltpu.CompilerParams(
            collective_id=0, has_side_effects=True, vmem_limit_bytes=48 * 2**20
        ),
        name="chain",
    )(start_panels[0], kinetic, fields)
    return orbits[None], logs[None]


def solution(mesh):
    placed = (P("tm", None, "inner"), P("inner", None), P("tm", None))
    return jax.shard_map(
        on_device,
        mesh=mesh,
        in_specs=placed,
        out_specs=(P("tm", None, None, "inner"), P("tm", None, None)),
        check_vma=False,
    )
```

```python
import functools
import math

import jax
import jax.numpy as jnp
from jax import lax
from jax.experimental import pallas as pl
from jax.experimental.pallas import tpu as pltpu
from jax.sharding import PartitionSpec as P

coupling = 0.17725
LANES = 128
B = 8


def contract(left, right, dims, precision):
    return lax.dot_general(
        left,
        right,
        (dims, ((), ())),
        precision=precision,
        preferred_element_type=jnp.float32,
    )


HIGHEST = lax.Precision.HIGHEST


def split_three(value):
    f32 = jnp.float32
    high = value.astype(jnp.bfloat16).astype(f32)
    middle = (value - high).astype(jnp.bfloat16).astype(f32)
    return high, middle, value - high - middle


def factor_into(work, columns, midway=None):
    r, width = work.shape
    tiles = width // LANES
    lane = lax.broadcasted_iota(jnp.int32, (1, LANES), 1)
    lane_all = lax.broadcasted_iota(jnp.int32, (1, width), 1)
    diagonal = [jnp.ones((1, LANES), jnp.float32) for _ in range(tiles)]
    for p in range(0, r, B):
        if midway is not None and p == (r * 7 // 8) // B * B:
            midway()
        home, off = p // LANES, p % LANES
        block = work[p : p + B, home * LANES : (home + 1) * LANES]
        for j in range(B):
            columns[j * B : (j + 1) * B, :] = jnp.broadcast_to(
                block[:, off + j : off + j + 1], (B, LANES)
            )
        d = [[columns[j * B + i : j * B + i + 1, :] for j in range(i + 1)] for i in range(B)]
        rows = []
        for t in range(B):
            parts = [work[p + t : p + t + 1, q * LANES : (q + 1) * LANES] for q in range(tiles)]
            unit = (lane == off + t).astype(jnp.float32)
            parts[home] = jnp.where((lane >= off) & (lane < off + B), unit, parts[home])
            rows.append(parts)
        for t in range(B):
            inverse = lax.rsqrt(d[t][t])
            diagonal[home] = jnp.where(lane == off + t, inverse, diagonal[home])
            below = [d[s][t] * inverse for s in range(t + 1, B)]
            for s in range(t + 1, B):
                for u in range(t + 1, s + 1):
                    d[s][u] = d[s][u] - below[s - t - 1] * below[u - t - 1]
            rows[t] = [part * inverse for part in rows[t]]
            for s in range(t + 1, B):
                rows[s] = [a - below[s - t - 1] * b for a, b in zip(rows[s], rows[t])]
        for t in range(B):
            for q in range(tiles):
                work[p + t : p + t + 1, q * LANES : (q + 1) * LANES] = rows[t][q]
        if p + B < r:
            pivot = work[p : p + B, :]
            high, middle, low = split_three(pivot)
            left = jnp.concatenate([high, high, middle, high, middle, low], axis=0)
            right = jnp.concatenate([high, middle, high, low, middle, high], axis=0)
            begin = (p + B) // 16 * 16
            turned = left.T[begin:r, :].astype(jnp.bfloat16)
            change = contract(turned, right.astype(jnp.bfloat16), ((1,), (0,)), None)
            change = change[p + B - begin :, :]
            rest = work[p + B : r, :]
            rest = jnp.where((lane_all >= p) & (lane_all < p + B), 0.0, rest)
            work[p + B : r, :] = rest - change
    return jnp.concatenate(diagonal, axis=1)


HIGH = lax.Precision.HIGH
MESH = pl.DeviceIdType.MESH


def split(value):
    high = value.astype(jnp.bfloat16)
    return high, (value - high.astype(jnp.float32)).astype(jnp.bfloat16)


def chain_kernel(
    n_tm,
    n_inner,
    hops,
    start,
    kinetic,
    fields_far,
    orbits,
    logs,
    full,
    panel,
    kin,
    kin_high,
    kin_low,
    fields,
    scales,
    stage,
    log_stage,
    log_in,
    moved,
    inverse,
    inverse_in,
    work,
    columns,
    ag_send,
    ag_recv,
    far_send,
    far_recv,
    local,
):
    r, rows = start.shape
    sites = n_inner * rows
    chips = n_inner // 2
    gain = math.sqrt(sites)
    last = hops - 1
    tm = lax.axis_index("tm")
    me = lax.axis_index("inner")
    chip, core = me // 2, me % 2
    sibling = chip * 2 + (1 - core)
    across = [((chip + d) % chips) * 2 + core for d in range(1, chips)]
    origin = [((chip + chips - d) % chips) * 2 + core for d in range(1, chips)]

    def ahead(distance):
        return lax.rem(tm + distance + n_tm, n_tm)

    offsets = sorted({d % n_tm for k in range(1, hops) for d in (k, -k)})
    barrier = pltpu.get_barrier_semaphore()
    for peer in [sibling] + across:
        pl.semaphore_signal(barrier, inc=1, device_id={"inner": peer}, device_id_type=MESH)
    for d in offsets:
        pl.semaphore_signal(barrier, inc=1, device_id={"tm": ahead(d)}, device_id_type=MESH)
    load_kin = pltpu.make_async_copy(kinetic, kin, local.at[0])
    load_kin.start()
    load_start = pltpu.make_async_copy(start, full.at[0, me], local.at[1])
    load_start.start()
    load_fields = pltpu.make_async_copy(fields_far, fields, local.at[2])
    load_fields.start()
    load_fields.wait()
    own_fields = fields[:, pl.ds(pl.multiple_of(me * rows, rows), rows)]
    scales[0] = jnp.broadcast_to(jnp.exp(coupling * own_fields.astype(jnp.float32)), (8, rows))
    load_start.wait()
    pl.semaphore_wait(barrier, chips + len(offsets))

    def send(source, target, sems, device):
        return pltpu.make_async_remote_copy(
            src_ref=source,
            dst_ref=target,
            send_sem=sems[0],
            recv_sem=sems[1],
            device_id=device,
            device_id_type=MESH,
        )

    def gather(g):
        def sems(i):
            return ag_send.at[g, i], ag_recv.at[g, i]

        def block(slot, i, device):
            return send(full.at[g, slot], full.at[g, slot], sems(i), {"inner": device})

        crossing = [block(me, d, across[d - 1]) for d in range(1, chips)]
        beside = block(me, 0, sibling)
        passed = [block(origin[d - 1], chips - 1 + d, sibling) for d in range(1, chips)]
        for copy in crossing:
            copy.start()
        beside.start()

        def forward():
            for copy, onward in zip(crossing, passed):
                copy.wait_recv()
                onward.start()

        def finish():
            beside.wait()
            for copy in crossing:
                copy.wait_send()
            for copy in passed:
                copy.wait()

        return forward, finish

    def far(kind, k):
        return far_send.at[kind, k], far_recv.at[kind, k]

    def mapped(blocks, hop):
        total = jnp.zeros((r, rows), jnp.float32)
        for j in range(n_inner):
            high, low = split(blocks[j])
            dims = ((1,), (0,))
            total += contract(high, kin_high[j], dims, None)
            total += contract(high, kin_low[j], dims, None)
            total += contract(low, kin_high[j], dims, None)
        return total * scales[hop][0:1, :]

    def gram_of(blocks):
        total = jnp.zeros((r, r), jnp.float32)
        for j in range(n_inner):
            block = blocks[j]
            total += contract(block, block, ((1,), (1,)), HIGHEST)
        return total

    below = lax.broadcasted_iota(jnp.int32, work.shape, 0) >= lax.broadcasted_iota(
        jnp.int32, work.shape, 1
    )

    half = r // 2
    part = pl.ds(pl.multiple_of(core * half, 8), half)

    pending = []
    forward, finish = gather(0)
    for k in range(1, hops):
        copy = send(scales.at[0], scales.at[k], far(0, k), {"tm": ahead(-k)})
        copy.start()
        pending.append(copy)
    load_kin.wait()
    for j in range(n_inner):
        turned = kin[:, j * rows : (j + 1) * rows].T
        kin_high[j], kin_low[j] = split(turned)
    forward()
    finish()
    full[1, me] = mapped(full.at[0], 0)
    forward, finish = gather(1)
    for copy in pending:
        copy.wait()
    pending = []
    forward()
    finish()

    blocks = full.at[1]
    work[...] = jnp.zeros_like(work)
    carried, shifted, told, swaps = [], [], [], []
    for hop in range(hops):
        there = {"tm": ahead(hop)}
        if hop < last:
            full[hop + 2, me] = mapped(blocks, hop + 1)
            forward, finish = gather(hop + 2)
        if hop > 0:
            stage[hop] = blocks[me]
            carried.append(send(stage.at[hop], moved.at[hop], far(1, hop), there))
            carried[-1].start()
        work[:, :r] = gram_of(blocks)
        diagonal = factor_into(work, columns, forward if hop < last else None)
        inverse[hop] = jnp.where(below, work[...], 0.0)
        log_stage[hop] = jnp.broadcast_to(-jnp.log(diagonal), log_stage.shape[1:])
        if hop > 0:
            source, target = inverse.at[hop, part], inverse_in.at[hop, part]
            shifted.append(send(source, target, far(2, hop), there))
            shifted[-1].start()
            told.append(send(log_stage.at[hop], log_in.at[hop], far(3, hop), there))
            told[-1].start()
        if hop < last:
            finish()
            for j in range(n_inner):
                panel[j] = contract(
                    inverse[hop][:, :r], full[hop + 2, j], ((1,), (0,)), HIGH
                )
            blocks = panel
    writes = []

    def write(hop, factor, block):
        moved[hop] = contract(gain * factor[:, :r], block, ((1,), (0,)), HIGH)
        writes.append(pltpu.make_async_copy(moved.at[hop], orbits.at[hop], local.at[3 + hop]))
        writes[-1].start()

    write(0, inverse[0], full[1, me])
    for group in (range(1, last), range(max(last, 1), hops)):
        for hop in group:
            shifted[hop - 1].wait_recv()
            half_in = inverse_in.at[hop, part]
            swaps.append(send(half_in, half_in, far(4, hop), {"inner": sibling}))
            swaps[-1].start()
        for hop in group:
            swaps[hop - 1].wait()
            carried[hop - 1].wait()
            write(hop, inverse_in[hop], moved[hop])
    for copy in shifted:
        copy.wait_send()
    for copy in told + writes:
        copy.wait()
    for hop in range(hops):
        held = log_stage if hop == 0 else log_in
        logs[hop : hop + 1, :] = held[hop][0:1, :r]


def on_device(start_panels, kinetic, fields):
    rows, sites = kinetic.shape
    r = start_panels.shape[1]
    n_tm, n_inner = lax.axis_size("tm"), lax.axis_size("inner")
    hops = n_tm // 2
    width = -(-r // LANES) * LANES
    f32, bf16 = jnp.float32, jnp.bfloat16
    vmem, far = pl.BlockSpec(memory_space=pltpu.VMEM), pl.BlockSpec(memory_space=pltpu.HBM)
    orbits, logs = pl.pallas_call(
        functools.partial(chain_kernel, n_tm, n_inner, hops),
        out_shape=(
            jax.ShapeDtypeStruct((hops, r, rows), f32),
            jax.ShapeDtypeStruct((hops, r), f32),
        ),
        in_specs=[far, far, far],
        out_specs=(far, vmem),
        scratch_shapes=[
            pltpu.VMEM((hops + 1, n_inner, r, rows), f32),
            pltpu.VMEM((n_inner, r, rows), f32),
            pltpu.VMEM((rows, sites), f32),
            pltpu.VMEM((n_inner, rows, rows), bf16),
            pltpu.VMEM((n_inner, rows, rows), bf16),
            pltpu.VMEM((1, sites), jnp.int32),
            pltpu.VMEM((hops, 8, rows), f32),
            pltpu.VMEM((hops, r, rows), f32),
            pltpu.VMEM((hops, 8, width), f32),
            pltpu.VMEM((hops, 8, width), f32),
            pltpu.VMEM((hops, r, rows), f32),
            pltpu.VMEM((hops, r, width), f32),
            pltpu.VMEM((hops, r, width), f32),
            pltpu.VMEM((r, width), f32),
            pltpu.VMEM((B * B, LANES), f32),
            pltpu.SemaphoreType.DMA((hops + 1, n_inner)),
            pltpu.SemaphoreType.DMA((hops + 1, n_inner)),
            pltpu.SemaphoreType.DMA((5, hops)),
            pltpu.SemaphoreType.DMA((5, hops)),
            pltpu.SemaphoreType.DMA((3 + hops,)),
        ],
        compiler_params=pltpu.CompilerParams(
            collective_id=0, has_side_effects=True, vmem_limit_bytes=56 * 2**20
        ),
        name="chain",
    )(start_panels[0], kinetic, fields)
    return orbits[None], logs[None]


def solution(mesh):
    placed = (P("tm", None, "inner"), P("inner", None), P("tm", None))
    return jax.shard_map(
        on_device,
        mesh=mesh,
        in_specs=placed,
        out_specs=(P("tm", None, None, "inner"), P("tm", None, None)),
        check_vma=False,
    )
```

```python
import functools
import math

import jax
import jax.numpy as jnp
from jax import lax
from jax.experimental import pallas as pl
from jax.experimental.pallas import tpu as pltpu
from jax.sharding import PartitionSpec as P

coupling = 0.17725
LANES = 128
B = 8


def contract(left, right, dims, precision):
    return lax.dot_general(
        left,
        right,
        (dims, ((), ())),
        precision=precision,
        preferred_element_type=jnp.float32,
    )


HIGHEST = lax.Precision.HIGHEST


def split_three(value):
    f32 = jnp.float32
    high = value.astype(jnp.bfloat16).astype(f32)
    middle = (value - high).astype(jnp.bfloat16).astype(f32)
    return high, middle, value - high - middle


def factor_into(work, columns, midway=None):
    r, width = work.shape
    tiles = width // LANES
    lane = lax.broadcasted_iota(jnp.int32, (1, LANES), 1)
    lane_all = lax.broadcasted_iota(jnp.int32, (1, width), 1)
    diagonal = [jnp.ones((1, LANES), jnp.float32) for _ in range(tiles)]
    for p in range(0, r, B):
        if midway is not None and p == (r * 7 // 8) // B * B:
            midway()
        home, off = p // LANES, p % LANES
        block = work[p : p + B, home * LANES : (home + 1) * LANES]
        for j in range(B):
            columns[j * B : (j + 1) * B, :] = jnp.broadcast_to(
                block[:, off + j : off + j + 1], (B, LANES)
            )
        d = [[columns[j * B + i : j * B + i + 1, :] for j in range(i + 1)] for i in range(B)]
        rows = []
        for t in range(B):
            parts = [work[p + t : p + t + 1, q * LANES : (q + 1) * LANES] for q in range(tiles)]
            unit = (lane == off + t).astype(jnp.float32)
            parts[home] = jnp.where((lane >= off) & (lane < off + B), unit, parts[home])
            rows.append(parts)
        for t in range(B):
            inverse = lax.rsqrt(d[t][t])
            diagonal[home] = jnp.where(lane == off + t, inverse, diagonal[home])
            below = [d[s][t] * inverse for s in range(t + 1, B)]
            for s in range(t + 1, B):
                for u in range(t + 1, s + 1):
                    d[s][u] = d[s][u] - below[s - t - 1] * below[u - t - 1]
            rows[t] = [part * inverse for part in rows[t]]
            for s in range(t + 1, B):
                rows[s] = [a - below[s - t - 1] * b for a, b in zip(rows[s], rows[t])]
        for t in range(B):
            for q in range(tiles):
                work[p + t : p + t + 1, q * LANES : (q + 1) * LANES] = rows[t][q]
        if p + B < r:
            pivot = work[p : p + B, :]
            high, middle, low = split_three(pivot)
            left = jnp.concatenate([high, high, middle, high, middle, low], axis=0)
            right = jnp.concatenate([high, middle, high, low, middle, high], axis=0)
            begin = (p + B) // 16 * 16
            turned = left.T[begin:r, :].astype(jnp.bfloat16)
            change = contract(turned, right.astype(jnp.bfloat16), ((1,), (0,)), None)
            change = change[p + B - begin :, :]
            rest = work[p + B : r, :]
            rest = jnp.where((lane_all >= p) & (lane_all < p + B), 0.0, rest)
            work[p + B : r, :] = rest - change
    return jnp.concatenate(diagonal, axis=1)


HIGH = lax.Precision.HIGH
MESH = pl.DeviceIdType.MESH


def split(value):
    high = value.astype(jnp.bfloat16)
    return high, (value - high.astype(jnp.float32)).astype(jnp.bfloat16)


def chain_kernel(
    n_tm,
    n_inner,
    hops,
    start,
    kinetic,
    fields_far,
    orbits,
    logs,
    full,
    panel,
    kin,
    kin_high,
    kin_low,
    fields,
    scales,
    stage,
    log_stage,
    log_in,
    moved,
    inverse,
    inverse_in,
    work,
    columns,
    ag_send,
    ag_recv,
    far_send,
    far_recv,
    local,
):
    r, rows = start.shape
    sites = n_inner * rows
    chips = n_inner // 2
    gain = math.sqrt(sites)
    last = hops - 1
    tm = lax.axis_index("tm")
    me = lax.axis_index("inner")
    chip, core = me // 2, me % 2
    sibling = chip * 2 + (1 - core)
    across = [((chip + d) % chips) * 2 + core for d in range(1, chips)]
    origin = [((chip + chips - d) % chips) * 2 + core for d in range(1, chips)]

    def ahead(distance):
        return lax.rem(tm + distance + n_tm, n_tm)

    offsets = sorted({d % n_tm for k in range(1, hops) for d in (k, -k)})
    barrier = pltpu.get_barrier_semaphore()
    for peer in [sibling] + across:
        pl.semaphore_signal(barrier, inc=1, device_id={"inner": peer}, device_id_type=MESH)
    for d in offsets:
        pl.semaphore_signal(barrier, inc=1, device_id={"tm": ahead(d)}, device_id_type=MESH)
    load_kin = pltpu.make_async_copy(kinetic, kin, local.at[0])
    load_kin.start()
    load_start = pltpu.make_async_copy(start, full.at[0, me], local.at[1])
    load_start.start()
    load_fields = pltpu.make_async_copy(fields_far, fields, local.at[2])
    load_fields.start()
    load_fields.wait()
    own_fields = fields[:, pl.ds(pl.multiple_of(me * rows, rows), rows)]
    scales[0] = jnp.broadcast_to(jnp.exp(coupling * own_fields.astype(jnp.float32)), (8, rows))
    load_start.wait()
    pl.semaphore_wait(barrier, chips + len(offsets))

    def send(source, target, sems, device):
        return pltpu.make_async_remote_copy(
            src_ref=source,
            dst_ref=target,
            send_sem=sems[0],
            recv_sem=sems[1],
            device_id=device,
            device_id_type=MESH,
        )

    def gather(g):
        def sems(i):
            return ag_send.at[g, i], ag_recv.at[g, i]

        def block(slot, i, device):
            return send(full.at[g, slot], full.at[g, slot], sems(i), {"inner": device})

        crossing = [block(me, d, across[d - 1]) for d in range(1, chips)]
        beside = block(me, 0, sibling)
        passed = [block(origin[d - 1], chips - 1 + d, sibling) for d in range(1, chips)]
        for copy in crossing:
            copy.start()
        beside.start()

        def forward():
            for copy, onward in zip(crossing, passed):
                copy.wait_recv()
                onward.start()

        def finish():
            beside.wait_send()
            for copy in crossing:
                copy.wait_send()
            for copy in passed:
                copy.wait()

        return beside.wait_recv, forward, finish

    def far(kind, k):
        return far_send.at[kind, k], far_recv.at[kind, k]

    def mapped_sum(blocks, order):
        total = jnp.zeros((r, rows), jnp.float32)
        for j in order:
            high, low = split(blocks[j])
            dims = ((1,), (0,))
            total += contract(high, kin_high[j], dims, None)
            total += contract(high, kin_low[j], dims, None)
            total += contract(low, kin_high[j], dims, None)
        return total

    def mapped(blocks, hop):
        return mapped_sum(blocks, range(n_inner)) * scales[hop][0:1, :]

    def gram_of(blocks):
        total = jnp.zeros((r, r), jnp.float32)
        for j in range(n_inner):
            block = blocks[j]
            total += contract(block, block, ((1,), (1,)), HIGHEST)
        return total

    below = lax.broadcasted_iota(jnp.int32, work.shape, 0) >= lax.broadcasted_iota(
        jnp.int32, work.shape, 1
    )

    half = r // 2
    part = pl.ds(pl.multiple_of(core * half, 8), half)

    pending = []
    near, forward, finish = gather(0)
    for k in range(1, hops):
        copy = send(scales.at[0], scales.at[k], far(0, k), {"tm": ahead(-k)})
        copy.start()
        pending.append(copy)
    load_kin.wait()
    for j in range(n_inner):
        turned = kin[:, j * rows : (j + 1) * rows].T
        kin_high[j], kin_low[j] = split(turned)
    near()
    total = mapped_sum(full.at[0], [me, sibling])
    forward()
    finish()
    rest = [c * 2 + u for c in [lax.rem(chip + d, chips) for d in range(1, chips)] for u in (0, 1)]
    full[1, me] = (total + mapped_sum(full.at[0], rest)) * scales[0][0:1, :]
    near, forward, finish = gather(1)
    for copy in pending:
        copy.wait()
    pending = []
    near()
    forward()
    finish()

    blocks = full.at[1]
    work[...] = jnp.zeros_like(work)
    carried, shifted, told, swaps = [], [], [], []
    for hop in range(hops):
        there = {"tm": ahead(hop)}
        if hop < last:
            full[hop + 2, me] = mapped(blocks, hop + 1)
            near, forward, finish = gather(hop + 2)
        if hop > 0:
            stage[hop] = blocks[me]
            carried.append(send(stage.at[hop], moved.at[hop], far(1, hop), there))
            carried[-1].start()
        work[:, :r] = gram_of(blocks)
        diagonal = factor_into(work, columns, forward if hop < last else None)
        inverse[hop] = jnp.where(below, work[...], 0.0)
        log_stage[hop] = jnp.broadcast_to(-jnp.log(diagonal), log_stage.shape[1:])
        if hop > 0:
            source, target = inverse.at[hop, part], inverse_in.at[hop, part]
            shifted.append(send(source, target, far(2, hop), there))
            shifted[-1].start()
            told.append(send(log_stage.at[hop], log_in.at[hop], far(3, hop), there))
            told[-1].start()
        if hop < last:
            near()
            finish()
            for j in range(n_inner):
                panel[j] = contract(
                    inverse[hop][:, :r], full[hop + 2, j], ((1,), (0,)), HIGH
                )
            blocks = panel
    writes = []

    def write(hop, factor, block):
        moved[hop] = contract(gain * factor[:, :r], block, ((1,), (0,)), HIGH)
        writes.append(pltpu.make_async_copy(moved.at[hop], orbits.at[hop], local.at[3 + hop]))
        writes[-1].start()

    write(0, inverse[0], full[1, me])
    for group in (range(1, last), range(max(last, 1), hops)):
        for hop in group:
            shifted[hop - 1].wait_recv()
            half_in = inverse_in.at[hop, part]
            swaps.append(send(half_in, half_in, far(4, hop), {"inner": sibling}))
            swaps[-1].start()
        for hop in group:
            swaps[hop - 1].wait()
            carried[hop - 1].wait()
            write(hop, inverse_in[hop], moved[hop])
    for copy in shifted:
        copy.wait_send()
    for copy in told + writes:
        copy.wait()
    for hop in range(hops):
        held = log_stage if hop == 0 else log_in
        logs[hop : hop + 1, :] = held[hop][0:1, :r]


def on_device(start_panels, kinetic, fields):
    rows, sites = kinetic.shape
    r = start_panels.shape[1]
    n_tm, n_inner = lax.axis_size("tm"), lax.axis_size("inner")
    hops = n_tm // 2
    width = -(-r // LANES) * LANES
    f32, bf16 = jnp.float32, jnp.bfloat16
    vmem, far = pl.BlockSpec(memory_space=pltpu.VMEM), pl.BlockSpec(memory_space=pltpu.HBM)
    orbits, logs = pl.pallas_call(
        functools.partial(chain_kernel, n_tm, n_inner, hops),
        out_shape=(
            jax.ShapeDtypeStruct((hops, r, rows), f32),
            jax.ShapeDtypeStruct((hops, r), f32),
        ),
        in_specs=[far, far, far],
        out_specs=(pl.BlockSpec(memory_space=pl.ANY), vmem),
        scratch_shapes=[
            pltpu.VMEM((hops + 1, n_inner, r, rows), f32),
            pltpu.VMEM((n_inner, r, rows), f32),
            pltpu.VMEM((rows, sites), f32),
            pltpu.VMEM((n_inner, rows, rows), bf16),
            pltpu.VMEM((n_inner, rows, rows), bf16),
            pltpu.VMEM((1, sites), jnp.int32),
            pltpu.VMEM((hops, 8, rows), f32),
            pltpu.VMEM((hops, r, rows), f32),
            pltpu.VMEM((hops, 8, width), f32),
            pltpu.VMEM((hops, 8, width), f32),
            pltpu.VMEM((hops, r, rows), f32),
            pltpu.VMEM((hops, r, width), f32),
            pltpu.VMEM((hops, r, width), f32),
            pltpu.VMEM((r, width), f32),
            pltpu.VMEM((B * B, LANES), f32),
            pltpu.SemaphoreType.DMA((hops + 1, n_inner)),
            pltpu.SemaphoreType.DMA((hops + 1, n_inner)),
            pltpu.SemaphoreType.DMA((5, hops)),
            pltpu.SemaphoreType.DMA((5, hops)),
            pltpu.SemaphoreType.DMA((3 + hops,)),
        ],
        compiler_params=pltpu.CompilerParams(
            collective_id=0, has_side_effects=True, vmem_limit_bytes=56 * 2**20
        ),
        name="chain",
    )(start_panels[0], kinetic, fields)
    return orbits[None], logs[None]


def solution(mesh):
    placed = (P("tm", None, "inner"), P("inner", None), P("tm", None))
    return jax.shard_map(
        on_device,
        mesh=mesh,
        in_specs=placed,
        out_specs=(P("tm", None, None, "inner"), P("tm", None, None)),
        check_vma=False,
    )
```
